256 devices in a mesh: dp: 32 (over y, z_hi, core), ctx: 8 (over x, z_lo).
Axes of the slice: x: 4, y: 4, z: 8 (z_hi: 4, z_lo: 2; z = z_hi * 2 + z_lo), core: 2. Of those that a mesh axis runs over, the one named last changes fastest.
Arguments:
- events: bfloat16 [65536, 512], P(('dp', 'ctx')), may hold values from -24 to 24
- out_grad: bfloat16 [65536, 512], P(('dp', 'ctx')), may hold values from -6 to 6
- proj_weight: bfloat16 [512, 2048], replicated, may hold values from -0.25 to 0.25
- out_weight: bfloat16 [512, 512], replicated, may hold values from -0.25 to 0.25
- lengths: int32 [32, 4], P('dp'), may hold values from 1 to 1024, 2048 in all within a row
- tile_mask: int32 [512, 16], P('dp'), may hold values 0 or 1
- quotient_shard: int32 [65536], P(('dp', 'ctx')), may hold values from 0 to 255, as said below
- quotient_row: int32 [65536], P(('dp', 'ctx')), may hold values from 0 to 65535
- remainder_shard: int32 [65536], P(('dp', 'ctx')), may hold values from 0 to 255, as said below
- remainder_row: int32 [65536], P(('dp', 'ctx')), may hold values from 0 to 65535
Outputs:
- quotient_grads: float32 [131072, 512], P(('dp', 'ctx'))
- remainder_grads: float32 [131072, 512], P(('dp', 'ctx'))
- proj_weight_grad: float32 [512, 2048], replicated
- out_weight_grad: float32 [512, 512], replicated
The draws below stay inside these ranges and needn't reach their ends.
Inputs may be any that keep to these rules, and one draw needn't show every extreme that they name: `quotient_shard`: in every device's 256 rows no shard is named more than 2 times, and some shard exactly 2 times. `remainder_shard`: in every device's 256 rows no shard is named more than 2 times, and some shard exactly 2 times.
All inputs are finite; a program needn't handle non-finite values. No bound on the sum of `tile_mask` on one device may be relied on, other than what follows from the above.
Results may differ from the reference program's by a relative error of at most 0.0068.
Values may be sent and summed in bfloat16 or wider, within the bound.
No kernel may reach another device: no remote copies, remote signals or barrier semaphores. Data moves between devices by JAX's collectives and lax.ppermute only.
A program may use at most 128 MiB of HBM per device.

```python
import math
import jax
import jax.numpy as jnp
import numpy as np
from jax import lax

D = 512
HEADS = 8
TILE = 128
HIST = 4
ROWS_DEV = 65536
TOK_DEV = 256
HD = 64
LEN = 2048
LMAX = 1024
NT = 16
TOKENS = 65536
CAP = 2
SLOTS = 512
N_DP = 32
DEVICES = 256


def shard_owners(key, salt_value):
    base_key = jax.random.fold_in(key, salt_value)
    slot_count = DEVICES * CAP

    def one_block(block_index):
        block_key = jax.random.fold_in(base_key, block_index)
        key_scores, key_forced, key_order = jax.random.split(block_key, 3)
        scores = jax.random.permutation(key_scores, slot_count)
        forced = jax.random.randint(key_forced, (), 0, DEVICES)
        slot_ids = jnp.arange(slot_count)
        scores = jnp.where(slot_ids // CAP == forced, -1 - slot_ids % CAP, scores)
        chosen = jnp.argsort(scores, stable=True)[:TOK_DEV]
        chosen = chosen[jax.random.permutation(key_order, TOK_DEV)]
        return (chosen // CAP).astype(jnp.int32)
    return jax.lax.map(one_block, jnp.arange(TOKENS // TOK_DEV)).reshape(TOKENS)


def draw_quotient_shard(key, part):
    return shard_owners(key, 17)


def draw_remainder_shard(key, part):
    return shard_owners(key, 29)


def set_ends(array, rng, low, high):
    index_at = [jax.random.randint(jax.random.fold_in(rng, axis), (), 0, length) for axis, length in enumerate(array.shape)]
    longest = array.shape.index(max(array.shape))
    neighbour = index_at[:longest] + [(index_at[longest] + 1) % array.shape[longest]] + index_at[longest + 1:]
    return array.at[tuple(index_at)].set(low).at[tuple(neighbour)].set(high)


def strengthened(values, stream_key, source, target, shards_of, factor):
    def block_of(dim):
        return (jnp.arange(values.shape[dim]) // (values.shape[dim] // shards_of)).reshape((-1,) + (1,) * (values.ndim - 1 - dim))

    one_side = jax.random.permutation(stream_key, shards_of)[block_of(target)]
    far = (block_of(target) + shards_of // 2) % shards_of
    return jnp.where((block_of(source) == one_side) | (block_of(source) == far), factor * values, values)


def block_scale(rng, extent, cuts, smallest, largest):
    def one(dim, shards_of):
        heights = jax.random.uniform(jax.random.fold_in(jax.random.fold_in(rng, 6), dim), (shards_of,), jnp.float32, smallest / len(cuts), largest / len(cuts))
        return jnp.repeat(jnp.exp(heights), extent[dim] // shards_of).reshape((-1,) + (1,) * (len(extent) - dim - 1))

    loudness = one(*cuts[0])
    for cut in cuts[1:]:
        loudness = loudness * one(*cut)
    return loudness


def cumulative_ranks(amount, lean):
    weights = [(1 << 20) // math.isqrt(rank ** lean) + 1 for rank in range(1, amount + 1)]
    deviation = 1 + sum(weights) // (1 << 30)
    return np.cumsum(np.array([max(1, weight // deviation) for weight in weights]))


def ranked(key, dims, count, lean):
    grid = cumulative_ranks(count, lean)
    pick = jax.random.randint(jax.random.fold_in(key, 1), dims, 0, int(grid[count - 1]))
    grade = jnp.searchsorted(jnp.asarray(grid, jnp.int32), pick, side="right")
    return jax.random.permutation(jax.random.fold_in(key, 2), count)[grade].astype(jnp.int32)


def profile(number_of, total, limit, slope):
    portions = [(1 << 20) // math.isqrt(rank ** slope) + 1 for rank in range(2, number_of + 1)]
    rest, given = total - limit - (number_of - 1), [1] * (number_of - 1)
    while rest > 0:
        candidates = [i for i in range(number_of - 1) if given[i] < limit]
        mass, remaining = sum([portions[i] for i in candidates]), rest
        for i in candidates:
            more = min(limit - given[i], max(1, remaining * portions[i] // mass), rest)
            given[i] = given[i] + more
            rest = rest - more
    return np.array([limit] + given)


def ragged_sizes(stream_key, amount, total, most, slope):
    if amount == 2:
        one = jax.random.randint(stream_key, (), max(1, total - most), min(most, total - 1) + 1)
        return jnp.stack([one, total - one])
    sizes = jnp.asarray(profile(amount, total, most, slope), jnp.int32)
    couples = (amount - 1) // 2
    donor, receiver = sizes[1:1 + 2 * couples:2], sizes[2:2 + 2 * couples:2]
    room = jnp.minimum(donor - 1, most - receiver)
    shifted = jax.random.randint(jax.random.fold_in(stream_key, 1), (couples,), 0, 1 << 20) % (room + 1)
    sizes = sizes.at[1:1 + 2 * couples:2].set(donor - shifted).at[2:2 + 2 * couples:2].set(receiver + shifted)
    return sizes[jax.random.permutation(jax.random.fold_in(stream_key, 2), amount)]


def bell_draw(stream_key, shape, spread, bound, cuts=(), kind=jnp.bfloat16):
    array = jax.random.normal(stream_key, shape, jnp.float32) * spread
    if len(cuts) > 0:
        array = block_scale(stream_key, shape, cuts, -0.22, 0.18) * array
    return jnp.clip(array, min=-bound, max=bound).astype(kind)


def noise_with(rng, dims, deviation, limit, cuts, heavy, kind=jnp.bfloat16):
    result = deviation * jax.random.normal(rng, dims, jnp.float32)
    if cuts:
        result = result * block_scale(rng, dims, cuts, -0.22, 0.18)
    return jnp.clip(strengthened(result, jax.random.fold_in(rng, 3), *heavy), -limit, limit).astype(kind)


def setup_inputs(seed: int = 0) -> dict:
    seeds = jax.random.split(jax.random.key(seed), 11)
    events = noise_with(seeds[0], (TOKENS, D), 1.0, 24.0, ((0, 256),), (0, 1, 256, 6.0))
    out_grad = bell_draw(seeds[1], (TOKENS, D), 1.0, 6.0, ((0, 256),))
    proj_weight = bell_draw(seeds[2], (D, 4 * D), D ** -0.5, 0.25)
    out_weight = bell_draw(seeds[3], (D, D), D ** -0.5, 0.25)
    lengths = jax.vmap(lambda own: ragged_sizes(own, HIST, LEN, LMAX, 0))(jax.random.split(seeds[4], N_DP)).reshape((N_DP, HIST)).astype(jnp.int32)
    tile_mask = set_ends((jax.random.randint(seeds[5], (N_DP * NT, NT), 0, 4) < 3).astype(jnp.int32), jax.random.fold_in(seeds[5], 1), 0, 1)
    quotient_shard = draw_quotient_shard(jax.random.fold_in(seeds[10], 71), 0)
    quotient_row = set_ends(ranked(seeds[7], (TOKENS,), ROWS_DEV, 2), jax.random.fold_in(seeds[7], 3), 0, ROWS_DEV - 1).astype(jnp.int32)
    remainder_shard = draw_remainder_shard(jax.random.fold_in(seeds[10], 71), 0)
    remainder_row = set_ends(ranked(seeds[9], (TOKENS,), ROWS_DEV, 2), jax.random.fold_in(seeds[9], 3), 0, ROWS_DEV - 1).astype(jnp.int32)
    return {"events": events, "out_grad": out_grad, "proj_weight": proj_weight, "out_weight": out_weight, "lengths": lengths, "tile_mask": tile_mask, "quotient_shard": quotient_shard, "quotient_row": quotient_row, "remainder_shard": remainder_shard, "remainder_row": remainder_row}


EPSILON = 1e-05

def silu_grad(value, sigma):
    return sigma * (1.0 + value * (1.0 - sigma))

def group_backward(packed_group, proj_weight, out_weight):
    inputs, cotangent, history, tile_table = packed_group
    score_scale = 1.0 / math.sqrt(HD)
    projected = jnp.dot(inputs, proj_weight, preferred_element_type=jnp.float32)
    sigmoid_proj = jax.nn.sigmoid(projected)
    activated = (projected * sigmoid_proj).astype(jnp.bfloat16)
    gate_rows = activated[:, :D].astype(jnp.float32)
    value_heads = activated[:, D:2 * D].astype(jnp.float32).reshape(LEN, HEADS, HD)
    query_heads = activated[:, 2 * D:3 * D].astype(jnp.float32).reshape(LEN, HEADS, HD)
    key_heads = activated[:, 3 * D:].astype(jnp.float32).reshape(LEN, HEADS, HD)
    position = jnp.arange(LEN, dtype=jnp.int32)
    doc_ends = jnp.cumsum(history)
    doc_ids = lax.optimization_barrier(jnp.sum((position[:, None] >= doc_ends[None, :]).astype(jnp.int32), axis=1))
    tile_full = jnp.repeat(jnp.repeat(tile_table, TILE, axis=0), TILE, axis=1)
    visible = (doc_ids[:, None] == doc_ids[None, :]) & (position[None, :] <= position[:, None]) & (tile_full == 1)
    weight = visible.astype(jnp.float32) / LMAX
    scores = jnp.einsum('ihd,jhd->hij', query_heads, key_heads) * score_scale
    sigmoid_scores = jax.nn.sigmoid(scores)
    attention = (scores * sigmoid_scores * weight[None]).astype(jnp.bfloat16).astype(jnp.float32)
    mixed_rows = jnp.einsum('hij,jhd->ihd', attention, value_heads).reshape(LEN, D)
    row_mean = lax.optimization_barrier(jnp.mean(mixed_rows, axis=1, keepdims=True))
    centered = mixed_rows - row_mean
    inv_scale = lax.rsqrt(lax.optimization_barrier(jnp.mean(centered * centered, axis=1, keepdims=True)) + EPSILON)
    normed = centered * inv_scale
    gated_rows = (normed * gate_rows).astype(jnp.bfloat16)
    out_weight_grad = jnp.dot(gated_rows.T, cotangent, preferred_element_type=jnp.float32)
    grad_gated = jnp.dot(cotangent, out_weight.T, preferred_element_type=jnp.float32)
    grad_normed = grad_gated * gate_rows
    grad_gate = grad_gated * normed
    grad_mixed = (inv_scale * (grad_normed - lax.optimization_barrier(jnp.mean(grad_normed, axis=1, keepdims=True)) - normed * lax.optimization_barrier(jnp.mean(grad_normed * normed, axis=1, keepdims=True)))).astype(jnp.bfloat16)
    grad_heads = grad_mixed.astype(jnp.float32).reshape(LEN, HEADS, HD)
    grad_attention = jnp.einsum('ihd,jhd->hij', grad_heads, value_heads)
    grad_scores = (grad_attention * weight[None] * silu_grad(scores, sigmoid_scores)).astype(jnp.bfloat16).astype(jnp.float32)
    grad_values = jnp.einsum('hij,ihd->jhd', attention, grad_heads).reshape(LEN, D)
    grad_query = jnp.einsum('hij,jhd->ihd', grad_scores, key_heads).reshape(LEN, D) * score_scale
    grad_keys = jnp.einsum('hij,ihd->jhd', grad_scores, query_heads).reshape(LEN, D) * score_scale
    grad_projected = (jnp.concatenate([grad_gate, grad_values, grad_query, grad_keys], axis=1) * silu_grad(projected, sigmoid_proj)).astype(jnp.bfloat16)
    grad_events = cotangent.astype(jnp.float32) + jnp.dot(grad_projected, proj_weight.T, preferred_element_type=jnp.float32)
    proj_weight_grad = jnp.dot(inputs.T, grad_projected, preferred_element_type=jnp.float32)
    return (grad_events, proj_weight_grad, out_weight_grad)

def route_rows(grad_events, shards, table_rows):
    owners = shards.reshape(DEVICES, TOK_DEV)
    earlier = jnp.arange(TOK_DEV)[None, :] < jnp.arange(TOK_DEV)[:, None]

    def block_rank(owner_block):
        matches = (owner_block[:, None] == owner_block[None, :]) & earlier
        return lax.optimization_barrier(jnp.sum(matches.astype(jnp.int32), axis=1)).astype(jnp.int32)
    slot_rank = lax.map(block_rank, owners).reshape(TOKENS)
    sender = (jnp.arange(TOKENS) // TOK_DEV).astype(jnp.int32)
    target = shards * SLOTS + sender * CAP + slot_rank
    buffer = jnp.zeros((DEVICES * SLOTS, D), jnp.float32).at[target].set(grad_events)
    labels = jnp.full((DEVICES * SLOTS,), -1, jnp.int32).at[target].set(table_rows)

    def owner_total(packed_owner):
        owner_block, row_marks = packed_owner
        matches = ((row_marks[:, None] == row_marks[None, :]) & (row_marks[None, :] >= 0)).astype(jnp.float32)
        return jnp.dot(matches, owner_block, precision=lax.Precision.HIGHEST, preferred_element_type=jnp.float32)
    totals = lax.map(owner_total, (buffer.reshape(DEVICES, SLOTS, D), labels.reshape(DEVICES, SLOTS)))
    return totals.reshape(DEVICES * SLOTS, D)

def reference(events, out_grad, proj_weight, out_weight, lengths, tile_mask, quotient_shard, quotient_row, remainder_shard, remainder_row):
    packed_groups = (events.reshape(N_DP, LEN, D), out_grad.reshape(N_DP, LEN, D), lengths, tile_mask.reshape(N_DP, NT, NT))
    grad_events, proj_parts, out_parts = lax.map(lambda packed_group: group_backward(packed_group, proj_weight, out_weight), packed_groups)
    grad_events = grad_events.reshape(TOKENS, D)
    quotient_grads = route_rows(grad_events, quotient_shard, quotient_row)
    remainder_grads = route_rows(grad_events, remainder_shard, remainder_row)
    return (quotient_grads, remainder_grads, lax.optimization_barrier(jnp.sum(proj_parts, axis=0)), lax.optimization_barrier(jnp.sum(out_parts, axis=0)))
```

```python
import math

import jax
import jax.numpy as jnp
from jax import lax
from jax.sharding import PartitionSpec as P

HEADS = 8
TILE = 128


EPSILON = 1e-05


def passed_along(shard, axis, by):
    count = lax.axis_size(axis)
    pairs = [(i, i + by) for i in range(count) if 0 <= i + by < count]
    return lax.ppermute(shard, axis, pairs)


def from_behind(shard, axis, by):
    count = lax.axis_size(axis)
    return lax.ppermute(shard, axis, [(i, (i + by) % count) for i in range(count)])


def silu_grad(value, sigma):
    return sigma * (1.0 + value * (1.0 - sigma))


def visible_weight(history, tile_table, row_start, row_count, col_start, col_count, longest):
    row_pos = row_start + jnp.arange(row_count, dtype=jnp.int32)
    col_pos = col_start + jnp.arange(col_count, dtype=jnp.int32)
    slots = jnp.arange(history.shape[0])
    doc_ends = jnp.sum(jnp.where(slots[None, :] <= slots[:, None], history[None, :], 0), axis=1)
    row_doc = jnp.sum((row_pos[:, None] >= doc_ends[None, :]).astype(jnp.int32), axis=1)
    col_doc = jnp.sum((col_pos[:, None] >= doc_ends[None, :]).astype(jnp.int32), axis=1)
    tile_ids = jnp.arange(tile_table.shape[0], dtype=jnp.int32)
    row_tiles = (row_pos[:, None] // TILE == tile_ids[None, :]).astype(jnp.float32)
    col_tiles = (col_pos[:, None] // TILE == tile_ids[None, :]).astype(jnp.float32)
    tile_rows = jnp.dot(row_tiles, tile_table.astype(jnp.float32), precision=lax.Precision.HIGHEST)
    tile_full = jnp.dot(tile_rows, col_tiles.T, precision=lax.Precision.HIGHEST)
    visible = (
        (row_doc[:, None] == col_doc[None, :])
        & (col_pos[None, :] <= row_pos[:, None])
        & (tile_full > 0.5)
    )
    return visible.astype(jnp.float32) / longest


def guarded(weight, compute, empty_result):
    return lax.cond(jnp.any(weight > 0.0), compute, lambda: empty_result)


def forward_block(query_heads, key_rows, value_rows, weight, score_scale):
    col_count = key_rows.shape[0]
    key_heads = key_rows.reshape(col_count, HEADS, -1)
    value_heads = value_rows.reshape(col_count, HEADS, -1)
    scores = (
        jnp.einsum("ihd,jhd->hij", query_heads, key_heads, preferred_element_type=jnp.float32)
        * score_scale
    )
    attention = (scores * jax.nn.sigmoid(scores) * weight[None]).astype(jnp.bfloat16)
    mixed_rows = jnp.einsum(
        "hij,jhd->ihd", attention, value_heads, preferred_element_type=jnp.float32
    )
    return mixed_rows.reshape(query_heads.shape[0], -1)


def backward_block(query_heads, grad_heads, key_rows, value_rows, weight, score_scale):
    col_count = key_rows.shape[0]
    row_count = query_heads.shape[0]
    key_heads = key_rows.reshape(col_count, HEADS, -1)
    value_heads = value_rows.reshape(col_count, HEADS, -1)
    scores = (
        jnp.einsum("ihd,jhd->hij", query_heads, key_heads, preferred_element_type=jnp.float32)
        * score_scale
    )
    sigmoid_scores = jax.nn.sigmoid(scores)
    attention = (scores * sigmoid_scores * weight[None]).astype(jnp.bfloat16)
    grad_attention = jnp.einsum(
        "ihd,jhd->hij", grad_heads, value_heads, preferred_element_type=jnp.float32
    )
    grad_scores = (grad_attention * weight[None] * silu_grad(scores, sigmoid_scores)).astype(
        jnp.bfloat16
    )
    grad_values = jnp.einsum(
        "hij,ihd->jhd", attention, grad_heads, preferred_element_type=jnp.float32
    ).reshape(col_count, -1)
    grad_query = (
        jnp.einsum(
            "hij,jhd->ihd", grad_scores, key_heads, preferred_element_type=jnp.float32
        ).reshape(row_count, -1)
        * score_scale
    )
    grad_keys = (
        jnp.einsum(
            "hij,ihd->jhd", grad_scores, query_heads, preferred_element_type=jnp.float32
        ).reshape(col_count, -1)
        * score_scale
    )
    return (grad_query, grad_keys, grad_values)


def pack_rows(grad_events, shards, table_rows, data_size, loop_size, capacity):
    row_count, model_width = grad_events.shape
    slot_count = data_size * loop_size * capacity
    earlier = jnp.arange(row_count)[None, :] < jnp.arange(row_count)[:, None]
    matches = (shards[:, None] == shards[None, :]) & earlier
    slot_rank = jnp.sum(matches.astype(jnp.int32), axis=1)
    target = shards * capacity + slot_rank
    onehot = jnp.arange(slot_count, dtype=jnp.int32)[:, None] == target[None, :]
    packed = jnp.dot(
        onehot.astype(jnp.float32),
        grad_events,
        precision=lax.Precision.HIGHEST,
        preferred_element_type=jnp.float32,
    )
    labels = jnp.sum(jnp.where(onehot, table_rows[None, :] + 1, 0), axis=1) - 1
    return (
        packed.reshape(data_size, loop_size, capacity, model_width),
        labels.reshape(data_size, loop_size, capacity),
    )


def merge_rows(received, row_marks):
    model_width = received.shape[-1]
    flat_rows = received.reshape(-1, model_width)
    flat_marks = row_marks.reshape(-1)
    matches = ((flat_marks[:, None] == flat_marks[None, :]) & (flat_marks[None, :] >= 0)).astype(
        jnp.float32
    )
    return jnp.dot(
        matches, flat_rows, precision=lax.Precision.HIGHEST, preferred_element_type=jnp.float32
    )


def body(
    events,
    out_grad,
    proj_weight,
    out_weight,
    lengths,
    tile_mask,
    quotient_shard,
    quotient_row,
    remainder_shard,
    remainder_row,
):
    row_count, model_width = events.shape
    loop_size = lax.axis_size("ctx")
    data_size = lax.axis_size("dp")
    loop_place = lax.axis_index("ctx")
    longest = float(row_count * loop_size // 2)
    score_scale = 1.0 / math.sqrt(model_width // HEADS)
    history = lengths[0]
    row_start = loop_place * row_count
    projected = jnp.dot(events, proj_weight, preferred_element_type=jnp.float32)
    sigmoid_proj = jax.nn.sigmoid(projected)
    activated = (projected * sigmoid_proj).astype(jnp.bfloat16)
    gate_rows = activated[:, :model_width].astype(jnp.float32)
    value_rows = activated[:, model_width : 2 * model_width]
    query_rows = activated[:, 2 * model_width : 3 * model_width]
    key_rows = activated[:, 3 * model_width :]
    query_heads = query_rows.reshape(row_count, HEADS, -1)
    empty_rows = jnp.zeros((row_count, model_width), jnp.float32)

    def forward_turn(turn_index, state):
        running, key_block, value_block = state
        offset_row = (loop_place - turn_index) % loop_size * row_count
        weight = visible_weight(
            history, tile_mask, row_start, row_count, offset_row, row_count, longest
        )
        running = running + guarded(
            weight,
            lambda: forward_block(query_heads, key_block, value_block, weight, score_scale),
            empty_rows,
        )
        key_next, value_next = passed_along((key_block, value_block), "ctx", 1)
        return (running, key_next, value_next)

    mixed_rows, key_spent, value_spent = lax.fori_loop(
        0, loop_size, forward_turn, (empty_rows, key_rows, value_rows)
    )
    row_mean = jnp.mean(mixed_rows, axis=1, keepdims=True)
    centered = mixed_rows - row_mean
    inv_scale = lax.rsqrt(jnp.mean(centered * centered, axis=1, keepdims=True) + EPSILON)
    normed = centered * inv_scale
    gated_rows = (normed * gate_rows).astype(jnp.bfloat16)
    out_weight_term = jnp.einsum(
        "td,te->de", gated_rows, out_grad, preferred_element_type=jnp.float32
    )
    grad_gated = jnp.einsum("te,de->td", out_grad, out_weight, preferred_element_type=jnp.float32)
    grad_normed = grad_gated * gate_rows
    grad_gate = grad_gated * normed
    grad_mixed = (
        inv_scale
        * (
            grad_normed
            - jnp.mean(grad_normed, axis=1, keepdims=True)
            - normed * jnp.mean(grad_normed * normed, axis=1, keepdims=True)
        )
    ).astype(jnp.bfloat16)
    grad_heads = grad_mixed.reshape(row_count, HEADS, -1)
    empty_triple = (empty_rows, empty_rows, empty_rows)

    def cycle_turn(turn_index, state):
        grad_query, key_block, value_block, key_grad_block, value_grad_block = state
        offset_row = (loop_place - turn_index) % loop_size * row_count
        weight = visible_weight(
            history, tile_mask, row_start, row_count, offset_row, row_count, longest
        )
        query_add, key_add, value_add = guarded(
            weight,
            lambda: backward_block(
                query_heads, grad_heads, key_block, value_block, weight, score_scale
            ),
            empty_triple,
        )
        key_next, value_next = passed_along((key_block, value_block), "ctx", 1)
        key_grad_next, value_grad_next = from_behind(
            (key_grad_block + key_add, value_grad_block + value_add), "ctx", 1
        )
        return (grad_query + query_add, key_next, value_next, key_grad_next, value_grad_next)

    grad_query, key_back, value_back, grad_keys, grad_values = lax.fori_loop(
        0, loop_size, cycle_turn, (empty_rows, key_rows, value_rows, empty_rows, empty_rows)
    )
    grad_projected = (
        jnp.concatenate([grad_gate, grad_values, grad_query, grad_keys], axis=1)
        * silu_grad(projected, sigmoid_proj)
    ).astype(jnp.bfloat16)
    grad_events = out_grad.astype(jnp.float32) + jnp.einsum(
        "tf,df->td", grad_projected, proj_weight, preferred_element_type=jnp.float32
    )
    proj_weight_term = jnp.einsum(
        "td,tf->df", events, grad_projected, preferred_element_type=jnp.float32
    )
    proj_weight_grad, out_weight_grad = lax.psum((proj_weight_term, out_weight_term), ("dp", "ctx"))
    devices = data_size * loop_size
    capacity = max(2, 3 * row_count // (2 * devices))
    quotient_buffer, quotient_labels = pack_rows(
        grad_events, quotient_shard, quotient_row, data_size, loop_size, capacity
    )
    remainder_buffer, remainder_labels = pack_rows(
        grad_events, remainder_shard, remainder_row, data_size, loop_size, capacity
    )
    quotient_in, remainder_in, quotient_marks, remainder_marks = (
        lax.all_to_all(
            lax.all_to_all(quotient_buffer, "dp", split_axis=0, concat_axis=0, tiled=True),
            "ctx",
            split_axis=1,
            concat_axis=1,
            tiled=True,
        ),
        lax.all_to_all(
            lax.all_to_all(remainder_buffer, "dp", split_axis=0, concat_axis=0, tiled=True),
            "ctx",
            split_axis=1,
            concat_axis=1,
            tiled=True,
        ),
        lax.all_to_all(
            lax.all_to_all(quotient_labels, "dp", split_axis=0, concat_axis=0, tiled=True),
            "ctx",
            split_axis=1,
            concat_axis=1,
            tiled=True,
        ),
        lax.all_to_all(
            lax.all_to_all(remainder_labels, "dp", split_axis=0, concat_axis=0, tiled=True),
            "ctx",
            split_axis=1,
            concat_axis=1,
            tiled=True,
        ),
    )
    quotient_grads = merge_rows(quotient_in, quotient_marks)
    remainder_grads = merge_rows(remainder_in, remainder_marks)
    return (quotient_grads, remainder_grads, proj_weight_grad, out_weight_grad)


def solution(mesh):
    in_specs = (
        P(("dp", "ctx"), None),
        P(("dp", "ctx"), None),
        P(),
        P(),
        P("dp", None),
        P("dp", None),
        P(("dp", "ctx")),
        P(("dp", "ctx")),
        P(("dp", "ctx")),
        P(("dp", "ctx")),
    )
    out_specs = (P(("dp", "ctx"), None), P(("dp", "ctx"), None), P(), P())
    return jax.shard_map(body, mesh=mesh, in_specs=in_specs, out_specs=out_specs, check_vma=False)
```

```python
import jax
import jax.numpy as jnp
from jax import lax
from jax.experimental import pallas as pl
from jax.experimental.pallas import tpu as pltpu
from jax.sharding import PartitionSpec as P

HEADS = 8
HD = 64
D = 512
TILE = 128
TOK = 256
LEN = 2048
NT = 16
NB = 8
LMAX = 1024
CAP = 2
DEVICES = 256
EPSILON = 1e-05
FAR = 1 << 30
BF = jnp.bfloat16
F32 = jnp.float32
MEMORY = 50 * 1024 * 1024

NN = (((1,), (0,)), ((), ()))
NT_DIMS = (((1,), (1,)), ((), ()))


def mm(a, b, dims=NN):
    return lax.dot_general(a, b, dims, preferred_element_type=F32)


def call(kernel, outs, scratch=(), smem=0, n_in=0):
    specs = [pl.BlockSpec(memory_space=pltpu.SMEM)] * smem + [
        pl.BlockSpec(memory_space=pltpu.VMEM)
    ] * (n_in - smem)
    return pl.pallas_call(
        kernel,
        out_shape=outs,
        in_specs=specs,
        out_specs=jax.tree.map(lambda _: pl.BlockSpec(memory_space=pltpu.VMEM), outs),
        scratch_shapes=list(scratch),
        compiler_params=pltpu.CompilerParams(vmem_limit_bytes=MEMORY),
    )


def out(shape, dtype):
    return jax.ShapeDtypeStruct(shape, dtype)


def send_kernel(ev_hbm, og_hbm, wo_hbm, out_ref, ev_s, og_s, wo_s, sems):
    copies = [
        pltpu.make_async_copy(src, dst, sems.at[i])
        for i, (src, dst) in enumerate(((og_hbm, og_s), (wo_hbm, wo_s), (ev_hbm, ev_s)))
    ]
    for copy in copies:
        copy.start()
    for copy in copies:
        copy.wait()
    gg = mm(wo_s[...], og_s[...], NT_DIMS).astype(BF)
    for h in range(HEADS):
        out_ref[h, :TOK, :] = ev_s[...]
        out_ref[h, TOK:, :TOK] = gg[HD * h : HD * h + 32]
        out_ref[h, TOK:, TOK:] = gg[HD * h + 32 : HD * h + 64]


def first_event(len_ref, position):
    e0 = len_ref[0]
    e1 = e0 + len_ref[1]
    e2 = e1 + len_ref[2]
    return jnp.where(
        position >= e2,
        e2,
        jnp.where(position >= e1, e1, jnp.where(position >= e0, e0, 0)),
    )


def seen(lo_ref, kb, k0, qs, row_pos):
    lower = jnp.concatenate(
        [
            jnp.broadcast_to(lo_ref[2 * kb, :, qs], (TILE, TOK)),
            jnp.broadcast_to(lo_ref[2 * kb + 1, :, qs], (TILE, TOK)),
        ],
        axis=0,
    )
    col_pos = k0 + lax.broadcasted_iota(jnp.int32, (TOK, TOK), 0)
    return (col_pos >= lower) & (col_pos <= row_pos)


def gate_cotangent(r_ref, s):
    return jnp.concatenate([r_ref[s, TOK:, :TOK], r_ref[s, TOK:, TOK:]], axis=0).astype(F32)


def forward_kernel(len_ref, r_ref, wt_ref, lo_ref, act_ref, ds_ref, mix_ref, out_ref, k_s, st_ref):
    for s in range(NB):
        cs = pl.ds(s * TOK, TOK)
        h = 0.5 * mm(wt_ref[...], r_ref[s, :TOK, :], NT_DIMS)
        t = jnp.tanh(h)
        u = h * t
        a = (h + u).astype(BF)
        act_ref[:, cs] = a
        ds_ref[:, cs] = (0.5 * (1.0 + t)) * (1.0 + (h - u))
        k_s[cs, :] = a[2 * HD : 3 * HD].T
    for qb in range(NB):
        qs = pl.ds(qb * TOK, TOK)
        qt = act_ref[:HD, qs] * BF(0.0625)
        row_pos = qb * TOK + lax.broadcasted_iota(jnp.int32, (1, TOK), 1)

        def step(kb, acc):
            k0 = pl.multiple_of(kb * TOK, TOK)
            h = mm(k_s[pl.ds(k0, TOK), :], qt)
            a = h + h * jnp.tanh(h)
            a = jnp.where(seen(lo_ref, kb, k0, qs, row_pos), a, 0.0).astype(BF)
            return acc + mm(act_ref[HD : 2 * HD, pl.ds(k0, TOK)], a)

        acc = lax.fori_loop(
            first_event(len_ref, qb * TOK) // TOK, qb + 1, step, jnp.zeros((HD, TOK), F32)
        )
        m = acc * (1.0 / LMAX)
        mix_ref[:, qs] = m
        s1 = jnp.sum(m, axis=0, keepdims=True)
        c = m - s1 * (1.0 / HD)
        gn = gate_cotangent(r_ref, qb) * act_ref[3 * HD :, qs].astype(F32)
        st_ref[0:1, qs] = s1
        st_ref[1:2, qs] = jnp.sum(c * c, axis=0, keepdims=True)
        st_ref[2:3, qs] = jnp.sum(gn, axis=0, keepdims=True)
        st_ref[3:4, qs] = jnp.sum(gn * c, axis=0, keepdims=True)
    for h in range(HEADS):
        out_ref[h] = st_ref[...]


def backward_kernel(
    len_ref, st_ref, r_ref, lo_ref, act_ref, ds_ref, mix_ref, lab_ref, gp_ref, gated_ref, k_s, v_s, dm_s, dv_s, dk_s
):
    gp_ref[:, 4 * HD :, :] = lab_ref[...]
    dv_s[...] = jnp.zeros((HD, LEN), F32)
    dk_s[...] = jnp.zeros((HD, LEN), F32)
    for s in range(NB):
        cs = pl.ds(s * TOK, TOK)
        v_s[cs, :] = act_ref[HD : 2 * HD, cs].T
        k_s[cs, :] = act_ref[2 * HD : 3 * HD, cs].T
        st = st_ref[:, :, cs]
        s1, m2, s3, s4 = st[:, 0], st[:, 1], st[:, 2], st[:, 3]
        mean = jnp.sum(s1, axis=0, keepdims=True) * (1.0 / D)
        apart = s1 * (1.0 / HD) - mean
        var = jnp.sum(m2 + HD * apart * apart, axis=0, keepdims=True) * (1.0 / D)
        inv = lax.rsqrt(var + EPSILON)
        mean_gn = jnp.sum(s3, axis=0, keepdims=True) * (1.0 / D)
        mean_gnn = jnp.sum(s4 + s3 * apart, axis=0, keepdims=True) * (1.0 / D) * inv
        normed = (mix_ref[:, cs] - mean) * inv
        gate = act_ref[3 * HD :, cs].astype(F32)
        gg = gate_cotangent(r_ref, s)
        gated_ref[:, cs] = (normed * gate).astype(BF)
        dm_s[:, cs] = (inv * (gg * gate - mean_gn - normed * mean_gnn)).astype(BF)
        gp_ref[s, 3 * HD : 4 * HD, :] = (gg * normed * ds_ref[3 * HD :, cs]).astype(BF)
    for qb in range(NB):
        qs = pl.ds(qb * TOK, TOK)
        qt = act_ref[:HD, qs] * BF(0.0625)
        dm = dm_s[:, qs]
        row_pos = qb * TOK + lax.broadcasted_iota(jnp.int32, (1, TOK), 1)

        def step(kb, acc):
            k0 = pl.multiple_of(kb * TOK, TOK)
            ks = pl.ds(k0, TOK)
            h = mm(k_s[ks, :], qt)
            da = mm(v_s[ks, :], dm)
            t = jnp.tanh(h)
            u = h * t
            vis = seen(lo_ref, kb, k0, qs, row_pos)
            a = jnp.where(vis, h + u, 0.0).astype(BF)
            d = jnp.where(vis, da * ((1.0 + t) * (1.0 + (h - u))), 0.0).astype(BF)
            dv_s[:, ks] += mm(dm, a, NT_DIMS)
            dk_s[:, ks] += mm(qt, d, NT_DIMS)
            return acc + mm(act_ref[2 * HD : 3 * HD, ks], d)

        acc = lax.fori_loop(
            first_event(len_ref, qb * TOK) // TOK, qb + 1, step, jnp.zeros((HD, TOK), F32)
        )
        gp_ref[qb, :HD, :] = (acc * (1.0 / (16 * LMAX)) * ds_ref[:HD, qs]).astype(BF)
    for s in range(NB):
        cs = pl.ds(s * TOK, TOK)
        gp_ref[s, HD : 2 * HD, :] = (dv_s[:, cs] * (1.0 / LMAX) * ds_ref[HD : 2 * HD, cs]).astype(BF)
        gp_ref[s, 2 * HD : 3 * HD, :] = (dk_s[:, cs] * (1.0 / LMAX) * ds_ref[2 * HD : 3 * HD, cs]).astype(BF)


def weight_kernel(place_ref, gp_ref, r_ref, gated_ref, *refs):
    ch_ref = refs[NB // 2]
    pw = jnp.zeros((4 * HD, D), F32)
    ow = jnp.zeros((HD, D), F32)
    for s in range(NB):
        pw = pw + mm(gp_ref[s, : 4 * HD], r_ref[s, :TOK, :])
        first = pl.multiple_of((place_ref[0] ^ s) * TOK, TOK)
        ow = ow + mm(gated_ref[:, pl.ds(first, TOK)], refs[s // 2][s % 2])
    pw = pw.T
    ch_ref[:D, :] = pw[:, :128]
    ch_ref[D : 2 * D, :] = pw[:, 128:]
    for c in range(4):
        ch_ref[2 * D + HD * c : 2 * D + HD * (c + 1), :] = ow[:, 128 * c : 128 * (c + 1)]


def pack_kernel(back_ref, w_ref, og_ref, tq_ref, tr_ref, out_ref, gp_s, row_s):
    for h in range(HEADS):
        for b, block in enumerate((2, 1, 3, 0)):
            gp_s[D * block + HD * h : D * block + HD * (h + 1), :] = back_ref[h, HD * b : HD * (b + 1), :]
    ge = (mm(w_ref[...], gp_s[...]).T + og_ref[...].astype(F32)).astype(BF)
    shard = lax.broadcasted_iota(jnp.int32, (DEVICES, TOK), 0)
    for t, target_ref in enumerate((tq_ref, tr_ref)):
        for k in range(CAP):
            pick = (target_ref[...] == CAP * shard + k).astype(F32).astype(BF)
            rows = mm(pick, ge)
            for c in range(4):
                row_s[pl.ds(8 * t + 4 * k + c, DEVICES, stride=16), :] = rows[:, 128 * c : 128 * (c + 1)]
    out_ref[...] = row_s[...].astype(BF).reshape(DEVICES, 16, 128)


def merge_kernel(in_ref, qc_ref, qr_ref, rc_ref, rr_ref, q_ref, r_ref, row_s):
    row_s[...] = in_ref[...].reshape(DEVICES * 16, 128).astype(F32)
    for t, (col_ref, mark_ref, o_ref) in enumerate(((qc_ref, qr_ref, q_ref), (rc_ref, rr_ref, r_ref))):
        same = (col_ref[...] == mark_ref[...]) & (mark_ref[...] >= 0)
        same = same.astype(F32).astype(BF)
        rows = jnp.concatenate(
            [
                jnp.concatenate(
                    [row_s[pl.ds(8 * t + 4 * k + c, DEVICES, stride=16), :] for c in range(4)], axis=1
                )
                for k in range(CAP)
            ],
            axis=0,
        ).astype(BF)
        o_ref[...] = mm(same, rows)


def place_kernel(place_ref, *refs):
    for k in range(HEADS):
        refs[HEADS][place_ref[0] ^ k] = refs[k][...]


def weights_out_kernel(core_ref, mine_ref, other_ref, pw_ref, ow_ref):
    step = pl.program_id(0)
    left = lax.broadcasted_iota(jnp.int32, (128, 128), 1) < HD

    def write(low_ref, high_ref):
        def write_part(part, get):
            low, high = ((2, 1), (3, 0))[part]
            for h in range(0, HEADS, 2):
                a, b = get(h), get(h + 1)
                pw_ref[:, D * low + HD * h : D * low + HD * h + 128] = jnp.where(left, a, pltpu.roll(b, HD, 1))
                pw_ref[:, D * high + HD * h : D * high + HD * h + 128] = jnp.where(left, pltpu.roll(a, HD, 1), b)

        first = pl.multiple_of(step * 128, 128)
        write_part(0, lambda h: low_ref[h, pl.ds(first, 128), :].astype(F32))

        @pl.when(step == 0)
        def _():
            write_part(1, lambda h: low_ref[h, D:640, :].astype(F32))

        @pl.when(step != 0)
        def _():
            after = pl.multiple_of(jnp.maximum(step - 1, 0) * 128, 128)
            write_part(1, lambda h: high_ref[h, pl.ds(after, 128), :].astype(F32))

        for i in range(2):
            for c in range(4):
                ow_ref[HD * i : HD * (i + 1), 128 * c : 128 * (c + 1)] = high_ref[
                    2 * step + i, 384 + HD * c : 384 + HD * (c + 1), :
                ].astype(F32)

    @pl.when(core_ref[0] == 0)
    def _():
        write(mine_ref, other_ref)

    @pl.when(core_ref[0] != 0)
    def _():
        write(other_ref, mine_ref)


def turned(stride, size, by, count=32):
    pairs = []
    for i in range(count):
        digit = (i // stride) % size
        pairs.append((i, i + ((digit + by) % size - digit) * stride))
    return pairs


def scatter_sum(x, stride):
    parts = x.reshape(4, x.shape[0] // 4, 128)
    me = (lax.axis_index("dp") // stride) % 4
    total = lax.dynamic_index_in_dim(parts, me, 0, False)
    for k in (1, 2, 3):
        sent = lax.dynamic_index_in_dim(parts, (me + k) % 4, 0, False)
        total = total + lax.ppermute(sent, "dp", turned(stride, 4, k))
    return total


def total(x, stride):
    return x + sum(lax.ppermute(x, "dp", turned(stride, 4, k)) for k in (1, 2, 3))


def by_source(parts, stride, size):
    me = (lax.axis_index("dp") // stride) % size
    held = [lax.dynamic_index_in_dim(parts, me, 0, False)]
    for k in range(1, size):
        sent = lax.dynamic_index_in_dim(parts, (me + k) % size, 0, False)
        held.append(lax.ppermute(sent, "dp", turned(stride, size, k)))
    back = jnp.stack([held[-i % size] for i in range(size)] * 2)
    return lax.dynamic_slice_in_dim(back, (size - me) % size, size, 0)


def gathered(x, stride):
    return by_source(jnp.broadcast_to(x[None], (4,) + x.shape), stride, 4).reshape(-1, 128)


def labels_over_dp(labels):
    x = labels.reshape(4, 4, 2, 32)
    x = by_source(x.transpose(2, 0, 1, 3), 1, 2)
    x = by_source(x.transpose(1, 0, 2, 3), 8, 4)
    x = by_source(x.transpose(2, 0, 1, 3), 2, 4)
    return x.transpose(1, 0, 2, 3)


def label_digits(x):
    x = x.reshape(32, 8, 4).transpose(1, 0, 2).reshape(8, 128)
    x = jnp.concatenate([(x + 1) // 256, (x + 1) % 256], axis=1)
    return jnp.broadcast_to(x[:, None], (8, 16, 256)).astype(BF)


def over_ctx(x, k):
    return lax.ppermute(x, "ctx", [(i, i ^ k) for i in range(8)])


def together(*arrays):
    return lax.optimization_barrier(arrays)


def core_sum(terms):
    core = lax.axis_index("dp") % 2
    halves = terms.reshape(2, 640, 128)
    mine = lax.dynamic_index_in_dim(halves, core, 0, False)
    other = lax.dynamic_index_in_dim(halves, 1 - core, 0, False)
    return mine + lax.ppermute(other, "dp", turned(1, 2, 1))


def weights_out(mine):
    core = lax.axis_index("dp") % 2
    other = lax.ppermute(mine, "dp", turned(1, 2, 1))
    whole = pl.BlockSpec((HEADS, 640, 128), lambda i: (0, 0, 0))
    return pl.pallas_call(
        weights_out_kernel,
        out_shape=(out((D, 4 * D), F32), out((D, D), F32)),
        grid=(4,),
        in_specs=[pl.BlockSpec(memory_space=pltpu.SMEM), whole, whole],
        out_specs=(pl.BlockSpec((128, 4 * D), lambda i: (i, 0)), pl.BlockSpec((128, D), lambda i: (i, 0))),
        compiler_params=pltpu.CompilerParams(vmem_limit_bytes=MEMORY),
    )(core.reshape(1).astype(jnp.int32), mine, other)


def slot_targets(shards):
    order = jnp.arange(TOK)
    earlier = (shards[:, None] == shards[None, :]) & (order[:, None] < order[None, :])
    return shards * CAP + jnp.sum(earlier.astype(jnp.int32), axis=0)


def slot_labels(target, rows):
    onehot = jnp.arange(DEVICES * CAP, dtype=jnp.int32)[:, None] == target[None, :]
    labels = jnp.sum(jnp.where(onehot, rows[None, :] + 1, 0), axis=1) - 1
    return labels.reshape(DEVICES, CAP)


def body(
    events,
    out_grad,
    proj_weight,
    out_weight,
    lengths,
    tile_mask,
    quotient_shard,
    quotient_row,
    remainder_shard,
    remainder_row,
):
    history = lengths[0]
    head = lax.axis_index("ctx")

    sent = pl.pallas_call(
        send_kernel,
        out_shape=out((HEADS, TOK + 32, D), BF),
        in_specs=[pl.BlockSpec(memory_space=pl.ANY)] * 3,
        out_specs=pl.BlockSpec(memory_space=pltpu.VMEM),
        scratch_shapes=[
            pltpu.VMEM((TOK, D), BF),
            pltpu.VMEM((TOK, D), BF),
            pltpu.VMEM((D, D), BF),
            pltpu.SemaphoreType.DMA((3,)),
        ],
        compiler_params=pltpu.CompilerParams(vmem_limit_bytes=MEMORY),
    )(events, out_grad, out_weight)
    sent, quotient_shard, remainder_shard = together(sent, quotient_shard, remainder_shard)
    received = lax.all_to_all(sent, "ctx", 0, 0, tiled=True)

    own = lax.dynamic_index_in_dim(proj_weight.reshape(D, 4, HEADS, HD), head, 2, False)
    own_t = jnp.stack([own[:, b].T for b in (2, 1, 3, 0)]).reshape(4 * HD, D)
    position = jnp.arange(LEN, dtype=jnp.int32)
    end0 = history[0]
    end1 = end0 + history[1]
    end2 = end1 + history[2]
    first = jnp.where(
        position >= end2,
        end2,
        jnp.where(position >= end1, end1, jnp.where(position >= end0, end0, 0)),
    )
    kept = jnp.repeat(tile_mask.T, TILE, axis=1) > 0
    lower = jnp.where(kept, first[None, :], FAR).reshape(NT, 1, LEN)

    quotient_target = slot_targets(quotient_shard)
    remainder_target = slot_targets(remainder_shard)
    labels = jnp.concatenate(
        [slot_labels(quotient_target, quotient_row), slot_labels(remainder_target, remainder_row)], axis=1
    )
    labels = labels_over_dp(labels)
    beside = over_ctx(out_grad, 1)
    received, beside = together(received, beside)
    grad_pair = jnp.stack([out_grad, beside])
    far_pair = over_ctx(grad_pair, 4)

    act, slope, mixed, stats = call(
        forward_kernel,
        (out((4 * HD, LEN), BF), out((4 * HD, LEN), F32), out((HD, LEN), F32), out((HEADS, 4, LEN), F32)),
        [pltpu.VMEM((LEN, HD), BF), pltpu.VMEM((4, LEN), F32)],
        smem=1,
        n_in=4,
    )(history, received, own_t, lower)
    stats, labels = together(stats, labels)
    all_stats = lax.all_to_all(stats, "ctx", 0, 0, tiled=True)
    labels = label_digits(labels)
    all_stats, grad_pair = together(all_stats, grad_pair)
    group_grad = [grad_pair, over_ctx(grad_pair, 2), far_pair, over_ctx(grad_pair, 6)]
    grads, gated = call(
        backward_kernel,
        (out((NB, 4 * HD + 16, TOK), BF), out((HD, LEN), BF)),
        [
            pltpu.VMEM((LEN, HD), BF),
            pltpu.VMEM((LEN, HD), BF),
            pltpu.VMEM((HD, LEN), BF),
            pltpu.VMEM((HD, LEN), F32),
            pltpu.VMEM((HD, LEN), F32),
        ],
        smem=1,
        n_in=8,
    )(history, all_stats, received, lower, act, slope, mixed, labels)
    grads, *group_grad = together(grads, *group_grad)

    back = lax.all_to_all(grads, "ctx", 0, 0, tiled=True)
    marks = back[:, 4 * HD].astype(F32).astype(jnp.int32)
    marks = marks[:, :128] * 256 + marks[:, 128:] - 1
    marks = marks.reshape(8, 32, 4).transpose(1, 0, 2).reshape(DEVICES, 2, CAP)
    terms = call(weight_kernel, out((1280, 128), F32), smem=1, n_in=8)(
        head.reshape(1).astype(jnp.int32), grads, received, gated, *group_grad
    )
    terms = scatter_sum(core_sum(terms), 8)
    back, terms = together(back, terms)
    terms = total(terms, 2)
    packed = call(
        pack_kernel,
        out((DEVICES, 16, 128), BF),
        [pltpu.VMEM((4 * D, TOK), BF), pltpu.VMEM((DEVICES * 16, 128), F32)],
        n_in=5,
    )(back, proj_weight, out_grad, quotient_target.reshape(1, TOK), remainder_target.reshape(1, TOK))
    packed, terms = together(packed, terms)
    arrived = lax.all_to_all(packed, ("dp", "ctx"), 0, 0, tiled=True)
    terms = gathered(terms, 8).astype(BF)
    columns = [marks[:, t].reshape(DEVICES * CAP, 1) for t in range(2)]
    rows = [marks[:, t].T.reshape(1, DEVICES * CAP) for t in range(2)]
    quotient_grads, remainder_grads = call(
        merge_kernel,
        (out((DEVICES * CAP, D), F32), out((DEVICES * CAP, D), F32)),
        [pltpu.VMEM((DEVICES * 16, 128), F32)],
        n_in=5,
    )(arrived, columns[0], rows[0], columns[1], rows[1])
    held = [terms] + [over_ctx(terms, k) for k in range(1, 8)]
    quotient_grads, *held = together(quotient_grads, *held)
    terms = call(place_kernel, out((HEADS, 640, 128), BF), smem=1, n_in=9)(head.reshape(1).astype(jnp.int32), *held)
    proj_weight_grad, out_weight_grad = weights_out(terms)
    return (quotient_grads, remainder_grads, proj_weight_grad, out_weight_grad)


def solution(mesh):
    split = P(("dp", "ctx"))
    in_specs = (
        P(("dp", "ctx"), None),
        P(("dp", "ctx"), None),
        P(),
        P(),
        P("dp", None),
        P("dp", None),
        split,
        split,
        split,
        split,
    )
    out_specs = (P(("dp", "ctx"), None), P(("dp", "ctx"), None), P(), P())
    return jax.shard_map(body, mesh=mesh, in_specs=in_specs, out_specs=out_specs, check_vma=False)
```

```python
import jax
import jax.numpy as jnp
from jax import lax
from jax.experimental import pallas as pl
from jax.experimental.pallas import tpu as pltpu
from jax.sharding import PartitionSpec as P

HEADS = 8
HD = 64
D = 512
TILE = 128
TOK = 256
LEN = 2048
NT = 16
NB = 8
QB = 512
QN = 4
LMAX = 1024
CAP = 2
DEVICES = 256
EPSILON = 1e-05
FAR = 1 << 30
BF = jnp.bfloat16
F32 = jnp.float32
MEMORY = 50 * 1024 * 1024
SMALL = 24 * 1024 * 1024

NN = (((1,), (0,)), ((), ()))
NT_DIMS = (((1,), (1,)), ((), ()))


def mm(a, b, dims=NN):
    return lax.dot_general(a, b, dims, preferred_element_type=F32)


def call(kernel, outs, scratch=(), smem=0, n_in=0, memory=MEMORY):
    specs = [pl.BlockSpec(memory_space=pltpu.SMEM)] * smem + [
        pl.BlockSpec(memory_space=pltpu.VMEM)
    ] * (n_in - smem)
    return pl.pallas_call(
        kernel,
        out_shape=outs,
        in_specs=specs,
        out_specs=jax.tree.map(lambda _: pl.BlockSpec(memory_space=pltpu.VMEM), outs),
        scratch_shapes=list(scratch),
        compiler_params=pltpu.CompilerParams(vmem_limit_bytes=memory),
    )


def out(shape, dtype):
    return jax.ShapeDtypeStruct(shape, dtype)


def send_kernel(ev_hbm, og_hbm, wo_hbm, out_ref, ev_s, og_s, wo_s, sems):
    copies = [
        pltpu.make_async_copy(src, dst, sems.at[i])
        for i, (src, dst) in enumerate(((og_hbm, og_s), (wo_hbm, wo_s), (ev_hbm, ev_s)))
    ]
    for copy in copies:
        copy.start()
    for copy in copies:
        copy.wait()
    gg = mm(wo_s[...], og_s[...], NT_DIMS).astype(BF)
    for h in range(HEADS):
        out_ref[h, :TOK, :] = ev_s[...]
        out_ref[h, TOK:, :TOK] = gg[HD * h : HD * h + 32]
        out_ref[h, TOK:, TOK:] = gg[HD * h + 32 : HD * h + 64]


def first_event(len_ref, position):
    e0 = len_ref[0]
    e1 = e0 + len_ref[1]
    e2 = e1 + len_ref[2]
    return jnp.where(
        position >= e2,
        e2,
        jnp.where(position >= e1, e1, jnp.where(position >= e0, e0, 0)),
    )


def seen(lo_ref, kb, k0, qs, row_pos):
    lower = jnp.concatenate(
        [
            jnp.broadcast_to(lo_ref[2 * kb, :, qs], (TILE, QB)),
            jnp.broadcast_to(lo_ref[2 * kb + 1, :, qs], (TILE, QB)),
        ],
        axis=0,
    )
    col_pos = k0 + lax.broadcasted_iota(jnp.int32, (TOK, QB), 0)
    return (col_pos >= lower) & (col_pos <= row_pos)


def gate_cotangent(r_ref, s):
    return jnp.concatenate([r_ref[s, TOK:, :TOK], r_ref[s, TOK:, TOK:]], axis=0).astype(F32)


def forward_kernel(len_ref, r_ref, wt_ref, lo_ref, act_ref, ds_ref, mix_ref, out_ref, k_s, st_ref):
    for s in range(NB):
        cs = pl.ds(s * TOK, TOK)
        h = 0.5 * mm(wt_ref[...], r_ref[s, :TOK, :], NT_DIMS)
        t = jnp.tanh(h)
        u = h * t
        a = (h + u).astype(BF)
        act_ref[:, cs] = a
        ds_ref[:, cs] = (0.5 * (1.0 + t)) * (1.0 + (h - u))
        k_s[cs, :] = a[2 * HD : 3 * HD].T
    for qb in range(QN):
        qs = pl.ds(qb * QB, QB)
        qt = act_ref[:HD, qs] * BF(0.0625)
        row_pos = qb * QB + lax.broadcasted_iota(jnp.int32, (1, QB), 1)

        def step(kb, acc):
            k0 = pl.multiple_of(kb * TOK, TOK)
            h = mm(k_s[pl.ds(k0, TOK), :], qt)
            a = h + h * jnp.tanh(h)
            a = jnp.where(seen(lo_ref, kb, k0, qs, row_pos), a, 0.0).astype(BF)
            return acc + mm(act_ref[HD : 2 * HD, pl.ds(k0, TOK)], a)

        acc = lax.fori_loop(
            first_event(len_ref, qb * QB) // TOK, (qb + 1) * (QB // TOK), step, jnp.zeros((HD, QB), F32)
        )
        m = acc * (1.0 / LMAX)
        mix_ref[:, qs] = m
        s1 = jnp.sum(m, axis=0, keepdims=True)
        c = m - s1 * (1.0 / HD)
        gn = jnp.concatenate([gate_cotangent(r_ref, s) for s in range(qb * QB // TOK, (qb + 1) * QB // TOK)], axis=1) * act_ref[3 * HD :, qs].astype(F32)
        st_ref[0:1, qs] = s1
        st_ref[1:2, qs] = jnp.sum(c * c, axis=0, keepdims=True)
        st_ref[2:3, qs] = jnp.sum(gn, axis=0, keepdims=True)
        st_ref[3:4, qs] = jnp.sum(gn * c, axis=0, keepdims=True)
    for h in range(HEADS):
        out_ref[h] = st_ref[...]


def backward_kernel(
    len_ref, st_ref, r_ref, lo_ref, act_ref, ds_ref, mix_ref, lab_ref, gp_ref, gated_ref, k_s, v_s, dm_s, dv_s, dk_s
):
    gp_ref[:, 4 * HD :, :] = lab_ref[...]
    dv_s[...] = jnp.zeros((HD, LEN), F32)
    dk_s[...] = jnp.zeros((HD, LEN), F32)
    for s in range(NB):
        cs = pl.ds(s * TOK, TOK)
        v_s[cs, :] = act_ref[HD : 2 * HD, cs].T
        k_s[cs, :] = act_ref[2 * HD : 3 * HD, cs].T
        st = st_ref[:, :, cs]
        s1, m2, s3, s4 = st[:, 0], st[:, 1], st[:, 2], st[:, 3]
        mean = jnp.sum(s1, axis=0, keepdims=True) * (1.0 / D)
        apart = s1 * (1.0 / HD) - mean
        var = jnp.sum(m2 + HD * apart * apart, axis=0, keepdims=True) * (1.0 / D)
        inv = lax.rsqrt(var + EPSILON)
        mean_gn = jnp.sum(s3, axis=0, keepdims=True) * (1.0 / D)
        mean_gnn = jnp.sum(s4 + s3 * apart, axis=0, keepdims=True) * (1.0 / D) * inv
        normed = (mix_ref[:, cs] - mean) * inv
        gate = act_ref[3 * HD :, cs].astype(F32)
        gg = gate_cotangent(r_ref, s)
        gated_ref[:, cs] = (normed * gate).astype(BF)
        dm_s[:, cs] = (inv * (gg * gate - mean_gn - normed * mean_gnn)).astype(BF)
        gp_ref[s, 3 * HD : 4 * HD, :] = (gg * normed * ds_ref[3 * HD :, cs]).astype(BF)
    for qb in range(QN):
        qs = pl.ds(qb * QB, QB)
        qt = act_ref[:HD, qs] * BF(0.0625)
        dm = dm_s[:, qs]
        row_pos = qb * QB + lax.broadcasted_iota(jnp.int32, (1, QB), 1)

        def step(kb, acc):
            k0 = pl.multiple_of(kb * TOK, TOK)
            ks = pl.ds(k0, TOK)
            h = mm(k_s[ks, :], qt)
            da = mm(v_s[ks, :], dm)
            t = jnp.tanh(h)
            u = h * t
            vis = seen(lo_ref, kb, k0, qs, row_pos)
            a = jnp.where(vis, h + u, 0.0).astype(BF)
            d = jnp.where(vis, da * ((1.0 + t) * (1.0 + (h - u))), 0.0).astype(BF)
            dv_s[:, ks] += mm(dm, a, NT_DIMS)
            dk_s[:, ks] += mm(qt, d, NT_DIMS)
            return acc + mm(act_ref[2 * HD : 3 * HD, ks], d)

        acc = lax.fori_loop(
            first_event(len_ref, qb * QB) // TOK, (qb + 1) * (QB // TOK), step, jnp.zeros((HD, QB), F32)
        )
        dq = (acc * (1.0 / (16 * LMAX)) * ds_ref[:HD, qs]).astype(BF)
        for i in range(QB // TOK):
            gp_ref[qb * (QB // TOK) + i, :HD, :] = dq[:, i * TOK : (i + 1) * TOK]
    for s in range(NB):
        cs = pl.ds(s * TOK, TOK)
        gp_ref[s, HD : 2 * HD, :] = (dv_s[:, cs] * (1.0 / LMAX) * ds_ref[HD : 2 * HD, cs]).astype(BF)
        gp_ref[s, 2 * HD : 3 * HD, :] = (dk_s[:, cs] * (1.0 / LMAX) * ds_ref[2 * HD : 3 * HD, cs]).astype(BF)


def weight_kernel(place_ref, gp_ref, r_ref, gated_ref, *refs):
    pair_ref, a_ref, far_a_ref, far_b_ref, b_ref, ch_ref = refs
    blocks = [pair_ref.at[0], pair_ref.at[1], a_ref.at[0], a_ref.at[1], far_a_ref, far_b_ref, b_ref.at[0], b_ref.at[1]]
    pw = jnp.zeros((4 * HD, D), F32)
    ow = jnp.zeros((HD, D), F32)
    for s in range(NB):
        pw = pw + mm(gp_ref[s, : 4 * HD], r_ref[s, :TOK, :])
        first = pl.multiple_of((place_ref[0] ^ s) * TOK, TOK)
        ow = ow + mm(gated_ref[:, pl.ds(first, TOK)], blocks[s][...])
    pw = pw.T
    ch_ref[:D, :] = pw[:, :128]
    ch_ref[D : 2 * D, :] = pw[:, 128:]
    for c in range(4):
        ch_ref[2 * D + HD * c : 2 * D + HD * (c + 1), :] = ow[:, 128 * c : 128 * (c + 1)]


def pack_kernel(back_ref, w_ref, og_ref, tq_ref, tr_ref, out_ref, gp_s, row_s):
    for h in range(HEADS):
        for b, block in enumerate((2, 1, 3, 0)):
            gp_s[D * block + HD * h : D * block + HD * (h + 1), :] = back_ref[h, HD * b : HD * (b + 1), :]
    ge = (mm(w_ref[...], gp_s[...]).T + og_ref[...].astype(F32)).astype(BF)
    shard = lax.broadcasted_iota(jnp.int32, (DEVICES, TOK), 0)
    for t, target_ref in enumerate((tq_ref, tr_ref)):
        for k in range(CAP):
            pick = (target_ref[...] == CAP * shard + k).astype(F32).astype(BF)
            rows = mm(pick, ge)
            for c in range(4):
                row_s[pl.ds(8 * t + 4 * k + c, DEVICES, stride=16), :] = rows[:, 128 * c : 128 * (c + 1)]
    out_ref[...] = row_s[...].astype(BF).reshape(DEVICES, 16, 128)


def merge_kernel(in_ref, qc_ref, qr_ref, rc_ref, rr_ref, q_ref, r_ref, row_s):
    row_s[...] = in_ref[...].reshape(DEVICES * 16, 128).astype(F32)
    for t, (col_ref, mark_ref, o_ref) in enumerate(((qc_ref, qr_ref, q_ref), (rc_ref, rr_ref, r_ref))):
        same = (col_ref[...] == mark_ref[...]) & (mark_ref[...] >= 0)
        same = same.astype(F32).astype(BF)
        rows = jnp.concatenate(
            [
                jnp.concatenate(
                    [row_s[pl.ds(8 * t + 4 * k + c, DEVICES, stride=16), :] for c in range(4)], axis=1
                )
                for k in range(CAP)
            ],
            axis=0,
        ).astype(BF)
        o_ref[...] = mm(same, rows)


def place_kernel(place_ref, y_ref, *refs):
    own_ref, a_ref, far_a_ref, far_b_ref, b_ref, out_ref = refs
    for j in range(4):
        first = pl.multiple_of((y_ref[0] ^ j) * 160, 32)
        for k in range(HEADS):
            if j == 2:
                piece = far_a_ref[k] if k < 4 else far_b_ref[k - 4]
            else:
                piece = (own_ref, a_ref, None, b_ref)[j][k]
            out_ref[place_ref[0] ^ k, pl.ds(first, 160), :] = piece


def weights_out_kernel(core_ref, mine_ref, other_ref, pw_ref, ow_ref):
    step = pl.program_id(0)
    left = lax.broadcasted_iota(jnp.int32, (128, 128), 1) < HD

    def write(low_ref, high_ref):
        def write_part(part, get):
            low, high = ((2, 1), (3, 0))[part]
            for h in range(0, HEADS, 2):
                a, b = get(h), get(h + 1)
                pw_ref[:, D * low + HD * h : D * low + HD * h + 128] = jnp.where(left, a, pltpu.roll(b, HD, 1))
                pw_ref[:, D * high + HD * h : D * high + HD * h + 128] = jnp.where(left, pltpu.roll(a, HD, 1), b)

        first = pl.multiple_of(step * 128, 128)
        write_part(0, lambda h: low_ref[h, pl.ds(first, 128), :].astype(F32))

        @pl.when(step == 0)
        def _():
            write_part(1, lambda h: low_ref[h, D:640, :].astype(F32))

        @pl.when(step != 0)
        def _():
            after = pl.multiple_of(jnp.maximum(step - 1, 0) * 128, 128)
            write_part(1, lambda h: high_ref[h, pl.ds(after, 128), :].astype(F32))

        for i in range(2):
            for c in range(4):
                ow_ref[HD * i : HD * (i + 1), 128 * c : 128 * (c + 1)] = high_ref[
                    2 * step + i, 384 + HD * c : 384 + HD * (c + 1), :
                ].astype(F32)

    @pl.when(core_ref[0] == 0)
    def _():
        write(mine_ref, other_ref)

    @pl.when(core_ref[0] != 0)
    def _():
        write(other_ref, mine_ref)


def turned(stride, size, by, count=32):
    pairs = []
    for i in range(count):
        digit = (i // stride) % size
        pairs.append((i, i + ((digit + by) % size - digit) * stride))
    return pairs


def scatter_sum(x, stride):
    parts = x.reshape(4, x.shape[0] // 4, 128)
    me = (lax.axis_index("dp") // stride) % 4
    total = lax.dynamic_index_in_dim(parts, me, 0, False)
    for k in (1, 2, 3):
        sent = lax.dynamic_index_in_dim(parts, (me + k) % 4, 0, False)
        total = total + lax.ppermute(sent, "dp", turned(stride, 4, k))
    return total


def over_z(x):
    return [lax.ppermute(x, "dp", turned(2, 4, k)) for k in (1, 2, 3)]


def to_source(parts, stride, size):
    me = (lax.axis_index("dp") // stride) % size
    held = [lax.dynamic_index_in_dim(parts, me, 0, False)]
    for k in range(1, size):
        sent = lax.dynamic_index_in_dim(parts, (me + k) % size, 0, False)
        held.append(lax.ppermute(sent, "dp", turned(stride, size, k)))
    return held


def by_source(held, stride):
    size = len(held)
    me = (lax.axis_index("dp") // stride) % size
    back = jnp.stack([held[-i % size] for i in range(size)] * 2)
    return lax.dynamic_slice_in_dim(back, (size - me) % size, size, 0)


def labels_over_dp(labels):
    x = labels.reshape(4, 4, 2, 32)
    x = by_source(to_source(x.transpose(2, 0, 1, 3), 1, 2), 1)
    x = by_source(to_source(x.transpose(1, 0, 2, 3), 8, 4), 8)
    return to_source(x.transpose(2, 0, 1, 3), 2, 4)


def label_digits(held):
    x = by_source(held, 2).transpose(1, 0, 2, 3)
    x = x.reshape(32, 8, 4).transpose(1, 0, 2).reshape(8, 128)
    x = jnp.concatenate([(x + 1) // 256, (x + 1) % 256], axis=1)
    return jnp.broadcast_to(x[:, None], (8, 16, 256)).astype(BF)


def over_y(x, k):
    return lax.ppermute(x, "dp", [(i, i ^ (8 * k)) for i in range(32)])


def over_ctx(x, k):
    return lax.ppermute(x, "ctx", [(i, i ^ k) for i in range(8)])


def together(*arrays):
    return lax.optimization_barrier(arrays)


def core_sum(terms):
    core = lax.axis_index("dp") % 2
    halves = terms.reshape(2, 640, 128)
    mine = lax.dynamic_index_in_dim(halves, core, 0, False)
    other = lax.dynamic_index_in_dim(halves, 1 - core, 0, False)
    return mine + lax.ppermute(other, "dp", turned(1, 2, 1))


def weights_out(mine):
    core = lax.axis_index("dp") % 2
    other = lax.ppermute(mine, "dp", turned(1, 2, 1))
    whole = pl.BlockSpec((HEADS, 640, 128), lambda i: (0, 0, 0))
    return pl.pallas_call(
        weights_out_kernel,
        out_shape=(out((D, 4 * D), F32), out((D, D), F32)),
        grid=(4,),
        in_specs=[pl.BlockSpec(memory_space=pltpu.SMEM), whole, whole],
        out_specs=(pl.BlockSpec((128, 4 * D), lambda i: (i, 0)), pl.BlockSpec((128, D), lambda i: (i, 0))),
        compiler_params=pltpu.CompilerParams(vmem_limit_bytes=MEMORY),
    )(core.reshape(1).astype(jnp.int32), mine, other)


def slot_targets(shards):
    order = jnp.arange(TOK)
    earlier = (shards[:, None] == shards[None, :]) & (order[:, None] < order[None, :])
    return shards * CAP + jnp.sum(earlier.astype(jnp.int32), axis=0)


def slot_labels(target, rows):
    onehot = jnp.arange(DEVICES * CAP, dtype=jnp.int32)[:, None] == target[None, :]
    labels = jnp.sum(jnp.where(onehot, rows[None, :] + 1, 0), axis=1) - 1
    return labels.reshape(DEVICES, CAP)


def body(
    events,
    out_grad,
    proj_weight,
    out_weight,
    lengths,
    tile_mask,
    quotient_shard,
    quotient_row,
    remainder_shard,
    remainder_row,
):
    history = lengths[0]
    head = lax.axis_index("ctx")

    sent = pl.pallas_call(
        send_kernel,
        out_shape=out((HEADS, TOK + 32, D), BF),
        in_specs=[pl.BlockSpec(memory_space=pl.ANY)] * 3,
        out_specs=pl.BlockSpec(memory_space=pltpu.VMEM),
        scratch_shapes=[
            pltpu.VMEM((TOK, D), BF),
            pltpu.VMEM((TOK, D), BF),
            pltpu.VMEM((D, D), BF),
            pltpu.SemaphoreType.DMA((3,)),
        ],
        compiler_params=pltpu.CompilerParams(vmem_limit_bytes=MEMORY),
    )(events, out_grad, out_weight)
    sent, quotient_shard, remainder_shard = together(sent, quotient_shard, remainder_shard)
    received = lax.all_to_all(sent, "ctx", 0, 0, tiled=True)

    own = lax.dynamic_index_in_dim(proj_weight.reshape(D, 4, HEADS, HD), head, 2, False)
    own_t = jnp.stack([own[:, b].T for b in (2, 1, 3, 0)]).reshape(4 * HD, D)
    position = jnp.arange(LEN, dtype=jnp.int32)
    end0 = history[0]
    end1 = end0 + history[1]
    end2 = end1 + history[2]
    first = jnp.where(
        position >= end2,
        end2,
        jnp.where(position >= end1, end1, jnp.where(position >= end0, end0, 0)),
    )
    kept = jnp.repeat(tile_mask.T, TILE, axis=1) > 0
    lower = jnp.where(kept, first[None, :], FAR).reshape(NT, 1, LEN)

    quotient_target = slot_targets(quotient_shard)
    remainder_target = slot_targets(remainder_shard)
    labels = jnp.concatenate(
        [slot_labels(quotient_target, quotient_row), slot_labels(remainder_target, remainder_row)], axis=1
    )
    labels = labels_over_dp(labels)
    beside = over_ctx(out_grad, 1)
    received, beside = together(received, beside)
    grad_pair = jnp.stack([out_grad, beside])
    near_a, near_b = over_ctx(grad_pair, 2), over_ctx(grad_pair, 6)

    act, slope, mixed, stats = call(
        forward_kernel,
        (out((4 * HD, LEN), BF), out((4 * HD, LEN), F32), out((HD, LEN), F32), out((HEADS, 4, LEN), F32)),
        [pltpu.VMEM((LEN, HD), BF), pltpu.VMEM((4, LEN), F32)],
        smem=1,
        n_in=4,
    )(history, received, own_t, lower)
    stats, *labels = together(stats, *labels)
    all_stats = lax.all_to_all(stats, "ctx", 0, 0, tiled=True)
    labels = label_digits(labels)
    all_stats, near_a, near_b = together(all_stats, near_a, near_b)
    group_grad = [grad_pair, near_a, over_ctx(near_a[0], 6), over_ctx(near_b[1], 2), near_b]
    grads, gated = call(
        backward_kernel,
        (out((NB, 4 * HD + 16, TOK), BF), out((HD, LEN), BF)),
        [
            pltpu.VMEM((LEN, HD), BF),
            pltpu.VMEM((LEN, HD), BF),
            pltpu.VMEM((HD, LEN), BF),
            pltpu.VMEM((HD, LEN), F32),
            pltpu.VMEM((HD, LEN), F32),
        ],
        smem=1,
        n_in=8,
    )(history, all_stats, received, lower, act, slope, mixed, labels)
    grads, *group_grad = together(grads, *group_grad)

    back = lax.all_to_all(grads, "ctx", 0, 0, tiled=True)
    marks = back[:, 4 * HD].astype(F32).astype(jnp.int32)
    marks = marks[:, :128] * 256 + marks[:, 128:] - 1
    marks = marks.reshape(8, 32, 4).transpose(1, 0, 2).reshape(DEVICES, 2, CAP)
    terms = call(weight_kernel, out((1280, 128), F32), smem=1, n_in=9)(
        head.reshape(1).astype(jnp.int32), grads, received, gated, *group_grad
    )
    terms = scatter_sum(core_sum(terms), 8)
    back, terms = together(back, terms)
    others = over_z(terms)
    packed = call(
        pack_kernel,
        out((DEVICES, 16, 128), BF),
        [pltpu.VMEM((4 * D, TOK), BF), pltpu.VMEM((DEVICES * 16, 128), F32)],
        n_in=5,
    )(back, proj_weight, out_grad, quotient_target.reshape(1, TOK), remainder_target.reshape(1, TOK))
    packed, *others = together(packed, *others)
    terms = (terms + sum(others)).astype(BF)
    terms = jnp.stack([terms, over_ctx(terms, 1)])
    packed, terms = together(packed, terms)
    arrived = lax.all_to_all(packed, ("dp", "ctx"), 0, 0, tiled=True)
    terms = jnp.concatenate([terms] + [over_ctx(terms, k) for k in (2, 4, 6)])
    y_a, y_b = over_y(terms, 1), over_y(terms, 3)
    held = [terms, y_a, over_y(y_a[:4], 3), over_y(y_b[4:], 1), y_b]
    columns = [marks[:, t].reshape(DEVICES * CAP, 1) for t in range(2)]
    rows = [marks[:, t].T.reshape(1, DEVICES * CAP) for t in range(2)]
    quotient_grads, remainder_grads = call(
        merge_kernel,
        (out((DEVICES * CAP, D), F32), out((DEVICES * CAP, D), F32)),
        [pltpu.VMEM((DEVICES * 16, 128), F32)],
        n_in=5,
    )(arrived, columns[0], rows[0], columns[1], rows[1])
    quotient_grads, *held = together(quotient_grads, *held)
    y_place = (lax.axis_index("dp") // 8).reshape(1).astype(jnp.int32)
    terms = call(place_kernel, out((HEADS, 640, 128), BF), smem=2, n_in=7, memory=SMALL)(
        head.reshape(1).astype(jnp.int32), y_place, *held
    )
    proj_weight_grad, out_weight_grad = weights_out(terms)
    return (quotient_grads, remainder_grads, proj_weight_grad, out_weight_grad)


def solution(mesh):
    split = P(("dp", "ctx"))
    in_specs = (
        P(("dp", "ctx"), None),
        P(("dp", "ctx"), None),
        P(),
        P(),
        P("dp", None),
        P("dp", None),
        split,
        split,
        split,
        split,
    )
    out_specs = (P(("dp", "ctx"), None), P(("dp", "ctx"), None), P(), P())
    return jax.shard_map(body, mesh=mesh, in_specs=in_specs, out_specs=out_specs, check_vma=False)
```

```python
import jax
import jax.numpy as jnp
from jax import lax
from jax.experimental import pallas as pl
from jax.experimental.pallas import tpu as pltpu
from jax.sharding import PartitionSpec as P

HEADS = 8
HD = 64
D = 512
TILE = 128
TOK = 256
LEN = 2048
NT = 16
NB = 8
QB = 512
QN = 4
LMAX = 1024
CAP = 2
DEVICES = 256
EPSILON = 1e-05
FAR = 1 << 30
BF = jnp.bfloat16
F32 = jnp.float32
MEMORY = 50 * 1024 * 1024
SMALL = 24 * 1024 * 1024

NN = (((1,), (0,)), ((), ()))
NT_DIMS = (((1,), (1,)), ((), ()))


def mm(a, b, dims=NN):
    return lax.dot_general(a, b, dims, preferred_element_type=F32)


def call(kernel, outs, scratch=(), smem=0, n_in=0, memory=MEMORY):
    specs = [pl.BlockSpec(memory_space=pltpu.SMEM)] * smem + [
        pl.BlockSpec(memory_space=pltpu.VMEM)
    ] * (n_in - smem)
    return pl.pallas_call(
        kernel,
        out_shape=outs,
        in_specs=specs,
        out_specs=jax.tree.map(lambda _: pl.BlockSpec(memory_space=pltpu.VMEM), outs),
        scratch_shapes=list(scratch),
        compiler_params=pltpu.CompilerParams(vmem_limit_bytes=memory),
    )


def out(shape, dtype):
    return jax.ShapeDtypeStruct(shape, dtype)


def send_kernel(ev_hbm, og_hbm, wo_hbm, out_ref, ev_s, og_s, wo_s, sems):
    copies = [
        pltpu.make_async_copy(src, dst, sems.at[i])
        for i, (src, dst) in enumerate(((og_hbm, og_s), (wo_hbm, wo_s), (ev_hbm, ev_s)))
    ]
    for copy in copies:
        copy.start()
    for copy in copies:
        copy.wait()
    gg = mm(wo_s[...], og_s[...], NT_DIMS).astype(BF)
    for h in range(HEADS):
        out_ref[h, :TOK, :] = ev_s[...]
        out_ref[h, TOK:, :TOK] = gg[HD * h : HD * h + 32]
        out_ref[h, TOK:, TOK:] = gg[HD * h + 32 : HD * h + 64]


def first_event(len_ref, position):
    e0 = len_ref[0]
    e1 = e0 + len_ref[1]
    e2 = e1 + len_ref[2]
    return jnp.where(
        position >= e2,
        e2,
        jnp.where(position >= e1, e1, jnp.where(position >= e0, e0, 0)),
    )


def seen(lo_ref, kb, k0, qs, row_pos):
    lower = jnp.concatenate(
        [
            jnp.broadcast_to(lo_ref[2 * kb, :, qs], (TILE, QB)),
            jnp.broadcast_to(lo_ref[2 * kb + 1, :, qs], (TILE, QB)),
        ],
        axis=0,
    )
    col_pos = k0 + lax.broadcasted_iota(jnp.int32, (TOK, QB), 0)
    return (col_pos >= lower) & (col_pos <= row_pos)


def gate_cotangent(r_ref, s):
    return jnp.concatenate([r_ref[s, TOK:, :TOK], r_ref[s, TOK:, TOK:]], axis=0).astype(F32)


def forward_kernel(len_ref, r_ref, wt_ref, lo_ref, act_ref, ds_ref, mix_ref, out_ref, k_s, st_ref):
    for s in range(NB):
        cs = pl.ds(s * TOK, TOK)
        h = 0.5 * mm(wt_ref[...], r_ref[s, :TOK, :], NT_DIMS)
        t = jnp.tanh(h)
        u = h * t
        a = (h + u).astype(BF)
        act_ref[:, cs] = a
        ds_ref[:, cs] = (0.5 * (1.0 + t)) * (1.0 + (h - u))
        k_s[cs, :] = a[2 * HD : 3 * HD].T
    for qb in range(QN):
        qs = pl.ds(qb * QB, QB)
        qt = act_ref[:HD, qs] * BF(0.0625)
        row_pos = qb * QB + lax.broadcasted_iota(jnp.int32, (1, QB), 1)

        def step(kb, acc):
            k0 = pl.multiple_of(kb * TOK, TOK)
            h = mm(k_s[pl.ds(k0, TOK), :], qt)
            a = h + h * jnp.tanh(h)
            a = jnp.where(seen(lo_ref, kb, k0, qs, row_pos), a, 0.0).astype(BF)
            return acc + mm(act_ref[HD : 2 * HD, pl.ds(k0, TOK)], a)

        acc = lax.fori_loop(
            first_event(len_ref, qb * QB) // TOK, (qb + 1) * (QB // TOK), step, jnp.zeros((HD, QB), F32)
        )
        m = acc * (1.0 / LMAX)
        mix_ref[:, qs] = m
        s1 = jnp.sum(m, axis=0, keepdims=True)
        c = m - s1 * (1.0 / HD)
        gn = jnp.concatenate([gate_cotangent(r_ref, s) for s in range(qb * QB // TOK, (qb + 1) * QB // TOK)], axis=1) * act_ref[3 * HD :, qs].astype(F32)
        st_ref[0:1, qs] = s1
        st_ref[1:2, qs] = jnp.sum(c * c, axis=0, keepdims=True)
        st_ref[2:3, qs] = jnp.sum(gn, axis=0, keepdims=True)
        st_ref[3:4, qs] = jnp.sum(gn * c, axis=0, keepdims=True)
    for h in range(HEADS):
        out_ref[h] = st_ref[...]


def backward_kernel(
    len_ref, st_ref, r_ref, lo_ref, act_ref, ds_ref, mix_ref, lab_ref, gp_ref, gated_ref, k_s, v_s, dm_s, dv_s, dk_s
):
    gp_ref[:, 4 * HD :, :] = lab_ref[...]
    dv_s[...] = jnp.zeros((HD, LEN), F32)
    dk_s[...] = jnp.zeros((HD, LEN), F32)
    for s in range(NB):
        cs = pl.ds(s * TOK, TOK)
        v_s[cs, :] = act_ref[HD : 2 * HD, cs].T
        k_s[cs, :] = act_ref[2 * HD : 3 * HD, cs].T
        st = st_ref[:, :, cs]
        s1, m2, s3, s4 = st[:, 0], st[:, 1], st[:, 2], st[:, 3]
        mean = jnp.sum(s1, axis=0, keepdims=True) * (1.0 / D)
        apart = s1 * (1.0 / HD) - mean
        var = jnp.sum(m2 + HD * apart * apart, axis=0, keepdims=True) * (1.0 / D)
        inv = lax.rsqrt(var + EPSILON)
        mean_gn = jnp.sum(s3, axis=0, keepdims=True) * (1.0 / D)
        mean_gnn = jnp.sum(s4 + s3 * apart, axis=0, keepdims=True) * (1.0 / D) * inv
        normed = (mix_ref[:, cs] - mean) * inv
        gate = act_ref[3 * HD :, cs].astype(F32)
        gg = gate_cotangent(r_ref, s)
        gated_ref[:, cs] = (normed * gate).astype(BF)
        dm_s[:, cs] = (inv * (gg * gate - mean_gn - normed * mean_gnn)).astype(BF)
        gp_ref[s, 3 * HD : 4 * HD, :] = (gg * normed * ds_ref[3 * HD :, cs]).astype(BF)
    for qb in range(QN):
        qs = pl.ds(qb * QB, QB)
        qt = act_ref[:HD, qs] * BF(0.0625)
        dm = dm_s[:, qs]
        row_pos = qb * QB + lax.broadcasted_iota(jnp.int32, (1, QB), 1)

        def step(kb, acc):
            k0 = pl.multiple_of(kb * TOK, TOK)
            ks = pl.ds(k0, TOK)
            h = mm(k_s[ks, :], qt)
            da = mm(v_s[ks, :], dm)
            t = jnp.tanh(h)
            u = h * t
            vis = seen(lo_ref, kb, k0, qs, row_pos)
            a = jnp.where(vis, h + u, 0.0).astype(BF)
            d = jnp.where(vis, da * ((1.0 + t) * (1.0 + (h - u))), 0.0).astype(BF)
            dv_s[:, ks] += mm(dm, a, NT_DIMS)
            dk_s[:, ks] += mm(qt, d, NT_DIMS)
            return acc + mm(act_ref[2 * HD : 3 * HD, ks], d)

        acc = lax.fori_loop(
            first_event(len_ref, qb * QB) // TOK, (qb + 1) * (QB // TOK), step, jnp.zeros((HD, QB), F32)
        )
        dq = (acc * (1.0 / (16 * LMAX)) * ds_ref[:HD, qs]).astype(BF)
        for i in range(QB // TOK):
            gp_ref[qb * (QB // TOK) + i, :HD, :] = dq[:, i * TOK : (i + 1) * TOK]
    for s in range(NB):
        cs = pl.ds(s * TOK, TOK)
        gp_ref[s, HD : 2 * HD, :] = (dv_s[:, cs] * (1.0 / LMAX) * ds_ref[HD : 2 * HD, cs]).astype(BF)
        gp_ref[s, 2 * HD : 3 * HD, :] = (dk_s[:, cs] * (1.0 / LMAX) * ds_ref[2 * HD : 3 * HD, cs]).astype(BF)


def weight_kernel(place_ref, gp_ref, r_ref, gated_ref, *refs):
    pair_ref, a_ref, far_a_ref, far_b_ref, b_ref, ch_ref = refs
    blocks = [pair_ref.at[0], pair_ref.at[1], a_ref.at[0], a_ref.at[1], far_a_ref, far_b_ref, b_ref.at[0], b_ref.at[1]]
    pw = jnp.zeros((4 * HD, D), F32)
    ow = jnp.zeros((HD, D), F32)
    for s in range(NB):
        pw = pw + mm(gp_ref[s, : 4 * HD], r_ref[s, :TOK, :])
        first = pl.multiple_of((place_ref[0] ^ s) * TOK, TOK)
        ow = ow + mm(gated_ref[:, pl.ds(first, TOK)], blocks[s][...])
    pw = pw.T
    ch_ref[:D, :] = pw[:, :128]
    ch_ref[D : 2 * D, :] = pw[:, 128:]
    for c in range(4):
        ch_ref[2 * D + HD * c : 2 * D + HD * (c + 1), :] = ow[:, 128 * c : 128 * (c + 1)]


def pack_kernel(back_ref, w_ref, og_ref, tq_ref, tr_ref, out_ref, gp_s, row_s):
    for h in range(HEADS):
        for b, block in enumerate((2, 1, 3, 0)):
            gp_s[D * block + HD * h : D * block + HD * (h + 1), :] = back_ref[h, HD * b : HD * (b + 1), :]
    ge = (mm(w_ref[...], gp_s[...]).T + og_ref[...].astype(F32)).astype(BF)
    shard = lax.broadcasted_iota(jnp.int32, (DEVICES, TOK), 0)
    for t, target_ref in enumerate((tq_ref, tr_ref)):
        for k in range(CAP):
            pick = (target_ref[...] == CAP * shard + k).astype(F32).astype(BF)
            rows = mm(pick, ge)
            for c in range(4):
                row_s[pl.ds(8 * t + 4 * k + c, DEVICES, stride=16), :] = rows[:, 128 * c : 128 * (c + 1)]
    out_ref[...] = row_s[...].astype(BF).reshape(DEVICES, 16, 128)


def merge_kernel(in_ref, qc_ref, qr_ref, rc_ref, rr_ref, q_ref, r_ref, row_s):
    row_s[...] = in_ref[...].reshape(DEVICES * 16, 128).astype(F32)
    for t, (col_ref, mark_ref, o_ref) in enumerate(((qc_ref, qr_ref, q_ref), (rc_ref, rr_ref, r_ref))):
        same = (col_ref[...] == mark_ref[...]) & (mark_ref[...] >= 0)
        same = same.astype(F32).astype(BF)
        rows = jnp.concatenate(
            [
                jnp.concatenate(
                    [row_s[pl.ds(8 * t + 4 * k + c, DEVICES, stride=16), :] for c in range(4)], axis=1
                )
                for k in range(CAP)
            ],
            axis=0,
        ).astype(BF)
        o_ref[...] = mm(same, rows)


def place_kernel(place_ref, y_ref, *refs):
    own_ref, a_ref, far_a_ref, far_b_ref, b_ref, out_ref = refs
    for j in range(4):
        first = pl.multiple_of((y_ref[0] ^ j) * 160, 32)
        for k in range(HEADS):
            if j == 2:
                piece = far_a_ref[k] if k < 4 else far_b_ref[k - 4]
            else:
                piece = (own_ref, a_ref, None, b_ref)[j][k]
            out_ref[place_ref[0] ^ k, pl.ds(first, 160), :] = piece


def weights_out_kernel(core_ref, mine_ref, other_ref, pw_ref, ow_ref):
    step = pl.program_id(0)
    left = lax.broadcasted_iota(jnp.int32, (128, 128), 1) < HD

    def write(low_ref, high_ref):
        def write_part(part, get):
            low, high = ((2, 1), (3, 0))[part]
            for h in range(0, HEADS, 2):
                a, b = get(h), get(h + 1)
                pw_ref[:, D * low + HD * h : D * low + HD * h + 128] = jnp.where(left, a, pltpu.roll(b, HD, 1))
                pw_ref[:, D * high + HD * h : D * high + HD * h + 128] = jnp.where(left, pltpu.roll(a, HD, 1), b)

        first = pl.multiple_of(step * 128, 128)
        write_part(0, lambda h: low_ref[h, pl.ds(first, 128), :].astype(F32))

        @pl.when(step == 0)
        def _():
            write_part(1, lambda h: low_ref[h, D:640, :].astype(F32))

        @pl.when(step != 0)
        def _():
            after = pl.multiple_of(jnp.maximum(step - 1, 0) * 128, 128)
            write_part(1, lambda h: high_ref[h, pl.ds(after, 128), :].astype(F32))

        for i in range(2):
            for c in range(4):
                ow_ref[HD * i : HD * (i + 1), 128 * c : 128 * (c + 1)] = high_ref[
                    2 * step + i, 384 + HD * c : 384 + HD * (c + 1), :
                ].astype(F32)

    @pl.when(core_ref[0] == 0)
    def _():
        write(mine_ref, other_ref)

    @pl.when(core_ref[0] != 0)
    def _():
        write(other_ref, mine_ref)


def turned(stride, size, by, count=32):
    pairs = []
    for i in range(count):
        digit = (i // stride) % size
        pairs.append((i, i + ((digit + by) % size - digit) * stride))
    return pairs


def scatter_sum(x, stride):
    parts = x.reshape(4, x.shape[0] // 4, 128)
    me = (lax.axis_index("dp") // stride) % 4
    total = lax.dynamic_index_in_dim(parts, me, 0, False)
    for k in (1, 2, 3):
        sent = lax.dynamic_index_in_dim(parts, (me + k) % 4, 0, False)
        total = total + lax.ppermute(sent, "dp", turned(stride, 4, k))
    return total


def over_z(x):
    return [lax.ppermute(x, "dp", turned(2, 4, k)) for k in (1, 2, 3)]


def to_source(parts, stride, size):
    me = (lax.axis_index("dp") // stride) % size
    held = [lax.dynamic_index_in_dim(parts, me, 0, False)]
    for k in range(1, size):
        sent = lax.dynamic_index_in_dim(parts, (me + k) % size, 0, False)
        held.append(lax.ppermute(sent, "dp", turned(stride, size, k)))
    return held


def by_source(held, stride):
    size = len(held)
    me = (lax.axis_index("dp") // stride) % size
    back = jnp.stack([held[-i % size] for i in range(size)] * 2)
    return lax.dynamic_slice_in_dim(back, (size - me) % size, size, 0)


def labels_over_dp(labels):
    x = labels.reshape(4, 4, 2, 32)
    x = by_source(to_source(x.transpose(2, 0, 1, 3), 1, 2), 1)
    x = by_source(to_source(x.transpose(1, 0, 2, 3), 8, 4), 8)
    return to_source(x.transpose(2, 0, 1, 3), 2, 4)


def label_digits(held):
    x = by_source(held, 2).transpose(1, 0, 2, 3)
    x = x.reshape(32, 8, 4).transpose(1, 0, 2).reshape(8, 128)
    x = jnp.concatenate([(x + 1) // 256, (x + 1) % 256], axis=1)
    return jnp.broadcast_to(x[:, None], (8, 16, 256)).astype(BF)


def over_y(x, k):
    return lax.ppermute(x, "dp", [(i, i ^ (8 * k)) for i in range(32)])


def over_ctx(x, k):
    return lax.ppermute(x, "ctx", [(i, i ^ k) for i in range(8)])


def together(*arrays):
    return lax.optimization_barrier(arrays)


def core_sum(terms):
    core = lax.axis_index("dp") % 2
    halves = terms.reshape(2, 640, 128)
    mine = lax.dynamic_index_in_dim(halves, core, 0, False)
    other = lax.dynamic_index_in_dim(halves, 1 - core, 0, False)
    return mine + lax.ppermute(other, "dp", turned(1, 2, 1))


def weights_out(mine):
    core = lax.axis_index("dp") % 2
    other = lax.ppermute(mine, "dp", turned(1, 2, 1))
    whole = pl.BlockSpec((HEADS, 640, 128), lambda i: (0, 0, 0))
    return pl.pallas_call(
        weights_out_kernel,
        out_shape=(out((D, 4 * D), F32), out((D, D), F32)),
        grid=(4,),
        in_specs=[pl.BlockSpec(memory_space=pltpu.SMEM), whole, whole],
        out_specs=(pl.BlockSpec((128, 4 * D), lambda i: (i, 0)), pl.BlockSpec((128, D), lambda i: (i, 0))),
        compiler_params=pltpu.CompilerParams(vmem_limit_bytes=MEMORY),
    )(core.reshape(1).astype(jnp.int32), mine, other)


def slot_targets(shards):
    order = jnp.arange(TOK)
    earlier = (shards[:, None] == shards[None, :]) & (order[:, None] < order[None, :])
    return shards * CAP + jnp.sum(earlier.astype(jnp.int32), axis=0)


def slot_labels(target, rows):
    onehot = jnp.arange(DEVICES * CAP, dtype=jnp.int32)[:, None] == target[None, :]
    labels = jnp.sum(jnp.where(onehot, rows[None, :] + 1, 0), axis=1) - 1
    return labels.reshape(DEVICES, CAP)


def body(
    events,
    out_grad,
    proj_weight,
    out_weight,
    lengths,
    tile_mask,
    quotient_shard,
    quotient_row,
    remainder_shard,
    remainder_row,
):
    history = lengths[0]
    head = lax.axis_index("ctx")

    sent = pl.pallas_call(
        send_kernel,
        out_shape=out((HEADS, TOK + 32, D), BF),
        in_specs=[pl.BlockSpec(memory_space=pl.ANY)] * 3,
        out_specs=pl.BlockSpec(memory_space=pltpu.VMEM),
        scratch_shapes=[
            pltpu.VMEM((TOK, D), BF),
            pltpu.VMEM((TOK, D), BF),
            pltpu.VMEM((D, D), BF),
            pltpu.SemaphoreType.DMA((3,)),
        ],
        compiler_params=pltpu.CompilerParams(vmem_limit_bytes=60 * 1024 * 1024),
    )(events, out_grad, out_weight)
    sent, quotient_shard, remainder_shard = together(sent, quotient_shard, remainder_shard)
    received = lax.all_to_all(sent, "ctx", 0, 0, tiled=True)

    own = lax.dynamic_index_in_dim(proj_weight.reshape(D, 4, HEADS, HD), head, 2, False)
    own_t = jnp.stack([own[:, b].T for b in (2, 1, 3, 0)]).reshape(4 * HD, D)
    position = jnp.arange(LEN, dtype=jnp.int32)
    end0 = history[0]
    end1 = end0 + history[1]
    end2 = end1 + history[2]
    first = jnp.where(
        position >= end2,
        end2,
        jnp.where(position >= end1, end1, jnp.where(position >= end0, end0, 0)),
    )
    kept = jnp.repeat(tile_mask.T, TILE, axis=1) > 0
    lower = jnp.where(kept, first[None, :], FAR).reshape(NT, 1, LEN)

    quotient_target = slot_targets(quotient_shard)
    remainder_target = slot_targets(remainder_shard)
    labels = jnp.concatenate(
        [slot_labels(quotient_target, quotient_row), slot_labels(remainder_target, remainder_row)], axis=1
    )
    labels = labels_over_dp(labels)
    beside = over_ctx(out_grad, 1)
    received, beside = together(received, beside)
    grad_pair = jnp.stack([out_grad, beside])
    near_a, near_b = over_ctx(grad_pair, 2), over_ctx(grad_pair, 6)

    act, slope, mixed, stats = call(
        forward_kernel,
        (out((4 * HD, LEN), BF), out((4 * HD, LEN), F32), out((HD, LEN), F32), out((HEADS, 4, LEN), F32)),
        [pltpu.VMEM((LEN, HD), BF), pltpu.VMEM((4, LEN), F32)],
        smem=1,
        n_in=4,
    )(history, received, own_t, lower)
    stats, *labels = together(stats, *labels)
    all_stats = lax.all_to_all(stats, "ctx", 0, 0, tiled=True)
    labels = label_digits(labels)
    all_stats, near_a, near_b = together(all_stats, near_a, near_b)
    group_grad = [grad_pair, near_a, over_ctx(near_a[0], 6), over_ctx(near_b[1], 2), near_b]
    grads, gated = call(
        backward_kernel,
        (out((NB, 4 * HD + 16, TOK), BF), out((HD, LEN), BF)),
        [
            pltpu.VMEM((LEN, HD), BF),
            pltpu.VMEM((LEN, HD), BF),
            pltpu.VMEM((HD, LEN), BF),
            pltpu.VMEM((HD, LEN), F32),
            pltpu.VMEM((HD, LEN), F32),
        ],
        smem=1,
        n_in=8,
    )(history, all_stats, received, lower, act, slope, mixed, labels)
    grads, *group_grad = together(grads, *group_grad)

    back = lax.all_to_all(grads, "ctx", 0, 0, tiled=True)
    marks = back[:, 4 * HD].astype(F32).astype(jnp.int32)
    marks = marks[:, :128] * 256 + marks[:, 128:] - 1
    marks = marks.reshape(8, 32, 4).transpose(1, 0, 2).reshape(DEVICES, 2, CAP)
    terms = call(weight_kernel, out((1280, 128), F32), smem=1, n_in=9)(
        head.reshape(1).astype(jnp.int32), grads, received, gated, *group_grad
    )
    terms = scatter_sum(core_sum(terms), 8)
    back, terms = together(back, terms)
    others = over_z(terms)
    packed = call(
        pack_kernel,
        out((DEVICES, 16, 128), BF),
        [pltpu.VMEM((4 * D, TOK), BF), pltpu.VMEM((DEVICES * 16, 128), F32)],
        n_in=5,
    )(back, proj_weight, out_grad, quotient_target.reshape(1, TOK), remainder_target.reshape(1, TOK))
    packed, *others = together(packed, *others)
    terms = (terms + sum(others)).astype(BF)
    terms = jnp.stack([terms, over_ctx(terms, 1)])
    packed, terms = together(packed, terms)
    arrived = lax.all_to_all(packed, ("dp", "ctx"), 0, 0, tiled=True)
    terms = jnp.concatenate([terms] + [over_ctx(terms, k) for k in (2, 4, 6)])
    y_a, y_b = over_y(terms, 1), over_y(terms, 3)
    held = [terms, y_a, over_y(y_a[:4], 3), over_y(y_b[4:], 1), y_b]
    columns = [marks[:, t].reshape(DEVICES * CAP, 1) for t in range(2)]
    rows = [marks[:, t].T.reshape(1, DEVICES * CAP) for t in range(2)]
    quotient_grads, remainder_grads = call(
        merge_kernel,
        (out((DEVICES * CAP, D), F32), out((DEVICES * CAP, D), F32)),
        [pltpu.VMEM((DEVICES * 16, 128), F32)],
        n_in=5,
    )(arrived, columns[0], rows[0], columns[1], rows[1])
    quotient_grads, *held = together(quotient_grads, *held)
    y_place = (lax.axis_index("dp") // 8).reshape(1).astype(jnp.int32)
    terms = call(place_kernel, out((HEADS, 640, 128), BF), smem=2, n_in=7, memory=SMALL)(
        head.reshape(1).astype(jnp.int32), y_place, *held
    )
    proj_weight_grad, out_weight_grad = weights_out(terms)
    return (quotient_grads, remainder_grads, proj_weight_grad, out_weight_grad)


def solution(mesh):
    split = P(("dp", "ctx"))
    in_specs = (
        P(("dp", "ctx"), None),
        P(("dp", "ctx"), None),
        P(),
        P(),
        P("dp", None),
        P("dp", None),
        split,
        split,
        split,
        split,
    )
    out_specs = (P(("dp", "ctx"), None), P(("dp", "ctx"), None), P(), P())
    return jax.shard_map(body, mesh=mesh, in_specs=in_specs, out_specs=out_specs, check_vma=False)
```
